32 devices in a mesh: cases: 2 (over y), vol: 4 (over z), ctrl: 4 (over x, core).
Axes of the slice: x: 2, y: 2, z: 4, core: 2. Of those that a mesh axis runs over, the one named last changes fastest.
Arguments:
- ctrl_coords: float32 [3, 65536], replicated, may hold values from 0 to 1536
- vol_coords: float32 [3, 524288], P(None, ('vol', 'ctrl')), may hold values from 0 to 1536
- sensitivity: float32 [3, 1048576], P(None, ('cases', 'vol', 'ctrl')), parts along dimension 1, may hold values from -0.3 to 0.3
- vol_lists: int32 [4096, 7], P(('vol', 'ctrl')), may hold values from -1 to 511, as said below
- ctrl_lists: int32 [512, 5], P(('vol', 'ctrl')), may hold values from -1 to 511, as said below
Outputs:
- solution: float32 [3, 131072], P(None, ('cases', 'vol', 'ctrl')), parts along dimension 1
- residual: float32 [3, 131072], P(None, ('cases', 'vol', 'ctrl')), parts along dimension 1
The draws below stay inside these ranges and needn't reach their ends.
There are 2 independent parts, one for each index of `cases`. The reference program is written for one: setup_inputs(seed, part) draws one part's arguments, and reference() takes and returns one part's arrays. A program takes and returns all parts, laid end to end along the dimension named above; an argument that names none is the same for every part. Nothing has to cross between parts.
Inputs may be any that keep to these rules, and one draw needn't show every extreme that they name: `vol_lists`: row v lists in increasing order the consecutive control tiles that may hold a point within distance 2 of a node of volume tile v, then -1 entries; every control tile holding such a point is listed. `ctrl_lists`: row t lists in increasing order the consecutive control tiles, t among them, that may hold a point within distance 2 of a point of tile t, then -1 entries; every live entry differs from t by at most 2, and the relation is symmetric.
All inputs are finite; a program needn't handle non-finite values.
Results may differ from the reference program's by a relative error of at most 0.0003.
Values sent between devices are 32-bit elements; how exact they have to be, the bound alone decides.
A program may use at most 128 MiB of HBM per device.

```python
import jax
import jax.numpy as jnp
from jax import lax

TILE = 128
NCTRL = 65536
NCT = 512
VT_DEV = 256
NVT = 4096
NVOL = 524288
KV = 7
KN = 5
ITERS = 2


def control_layout(key):
    lengths = jax.random.randint(jax.random.fold_in(key, 101), (NCT,), 1, 4).astype(jnp.int32)
    ends = jnp.cumsum(lengths).astype(jnp.int32)
    return (ends - lengths, lengths, ends)


def volume_layout(key):
    starts, lengths, ends = control_layout(key)
    device = jnp.arange(NVT, dtype=jnp.int32) // VT_DEV
    spread = jax.random.randint(jax.random.fold_in(key, 102), (NVT,), 0, 3).astype(jnp.int32)
    spans = (1 + spread % (1 + device % 3)).astype(jnp.int32)
    anchor = jax.random.randint(jax.random.fold_in(key, 103), (NVT,), 0, ends[-1] - 3).astype(jnp.int32)
    return (starts, ends, anchor, spans)


def tile_list(starts, ends, lower, upper, width):
    first = jnp.searchsorted(ends, lower, side='right').astype(jnp.int32)
    wanted = first[:, None] + jnp.arange(width, dtype=jnp.int32)[None, :]
    safe = jnp.clip(wanted, 0, NCT - 1)
    keep = (wanted < NCT) & (starts[safe] < upper[:, None])
    return jnp.where(keep, wanted, -1).astype(jnp.int32)


def draw_ctrl_coords(key, part):
    starts, lengths, ends = control_layout(key)
    key = jax.random.fold_in(key, 1)
    unit = jax.random.uniform(key, (3, NCT, TILE), jnp.float32)
    along = starts[:, None].astype(jnp.float32) + lengths[:, None].astype(jnp.float32) * unit[0]
    return jnp.stack([along, unit[1], unit[2]]).reshape(3, NCTRL)


def draw_vol_coords(key, part):
    starts, ends, anchor, spans = volume_layout(key)
    key = jax.random.fold_in(key, 2)
    unit = jax.random.uniform(key, (3, NVT, TILE), jnp.float32)
    along = anchor[:, None].astype(jnp.float32) + spans[:, None].astype(jnp.float32) * unit[0]
    return jnp.stack([along, unit[1], unit[2]]).reshape(3, NVOL)


def draw_vol_lists(key, part):
    starts, ends, anchor, spans = volume_layout(key)
    return tile_list(starts, ends, anchor - 2, anchor + spans + 2, KV)


def draw_ctrl_lists(key, part):
    starts, lengths, ends = control_layout(key)
    return tile_list(starts, ends, starts - 2, ends + 2, KN)


def levels(stream_key, dims, cuts, least, high):
    gain, own = 1.0, jax.random.fold_in(stream_key, 6)
    for position, shards_of in cuts:
        steps = jnp.exp(jax.random.uniform(jax.random.fold_in(own, position), (shards_of,), jnp.float32, least / len(cuts), high / len(cuts)))
        gain = gain * jnp.repeat(steps, dims[position] // shards_of).reshape([-1 if axis == position else 1 for axis in range(len(dims))])
    return gain


def noise(key, extent, scale, bound, pieces=(), kind=jnp.bfloat16):
    values = scale * jax.random.normal(key, extent, jnp.float32)
    if pieces:
        values = values * levels(key, extent, pieces, -0.22, 0.18)
    return jnp.clip(values, -bound, bound).astype(kind)


def setup_inputs(seed: int = 0, part: int = 0) -> dict:
    seeds = jax.random.split(jax.random.key(seed), 6)
    own_keys = jax.random.split(jax.random.fold_in(seeds[5], part), 6)
    return {
        "ctrl_coords": draw_ctrl_coords(jax.random.fold_in(seeds[5], 71), part),
        "vol_coords": draw_vol_coords(jax.random.fold_in(seeds[5], 71), part),
        "sensitivity": noise(own_keys[2], (3, NVOL), 0.05, 0.3, ((1, 16),), jnp.float32),
        "vol_lists": draw_vol_lists(jax.random.fold_in(seeds[5], 71), part),
        "ctrl_lists": draw_ctrl_lists(jax.random.fold_in(seeds[5], 71), part),
    }


support_radius = 2.0
diagonal_shift = 1.0
kernel_weight = 0.03125
high = lax.Precision.HIGHEST

def wendland(ctrl_pts, vol_pts):
    square = sum(((ctrl_pts[i][..., :, None] - vol_pts[i][..., None, :]) ** 2 for i in range(3)))
    ratio = jnp.sqrt(square) / support_radius
    margin = jnp.maximum(1.0 - ratio, 0.0)
    return margin ** 4 * (4.0 * ratio + 1.0)

def transpose_group(carry, item, ctrl_tiles):
    points, grads, ids = item
    live = ids >= 0
    safe = jnp.clip(ids, 0, ctrl_tiles.shape[1] - 1).astype(jnp.int32)
    near = ctrl_tiles[:, safe, :]
    kern = wendland(near, points[:, :, None, :])
    kern = jnp.where(live[:, :, None, None], kern, 0.0)
    contrib = jnp.einsum('gkcv,dgv->dgkc', kern, grads, precision=high)
    return carry.at[:, safe.reshape(-1), :].add(contrib.reshape(3, -1, contrib.shape[-1]))

def control_kernels(ctrl_tiles, own_tiles, lists):
    safe = jnp.clip(lists, 0, ctrl_tiles.shape[1] - 1).astype(jnp.int32)
    near = ctrl_tiles[:, safe, :]
    kern = wendland(own_tiles[:, :, None, :], near)
    return jnp.where((lists >= 0)[:, :, None, None], kern, 0.0)

def reference(ctrl_coords, vol_coords, sensitivity, vol_lists, ctrl_lists):
    ctrl_tiles = ctrl_coords.reshape(3, NCT, TILE)
    group = 64
    turns = NVT // group
    points = vol_coords.reshape(3, turns, group, TILE).transpose(1, 0, 2, 3)
    grads = sensitivity.reshape(3, turns, group, TILE).transpose(1, 0, 2, 3)
    ids = vol_lists.reshape(turns, group, KV)

    def visit_group(carry, item):
        return (transpose_group(carry, item, ctrl_tiles), None)
    load, unused = lax.scan(visit_group, jnp.zeros((3, NCT, TILE), jnp.float32), (points, grads, ids))
    load = load.reshape(3, NCTRL)
    kern = control_kernels(ctrl_tiles, ctrl_tiles, ctrl_lists)
    safe = jnp.clip(ctrl_lists, 0, NCT - 1).astype(jnp.int32)

    def operate(field):
        tiles = field.reshape(3, NCT, TILE)
        near = tiles[:, safe, :]
        mixed = jnp.einsum('ckrv,dckv->dcr', kern, near, precision=high)
        return diagonal_shift * field + kernel_weight * mixed.reshape(3, NCTRL)
    solution = jnp.zeros_like(load)
    residual = load
    direction = load
    norm_now = jnp.sum(residual * residual)
    for step in range(ITERS):
        image = operate(direction)
        alpha = norm_now / jnp.sum(direction * image)
        solution = solution + alpha * direction
        residual = residual - alpha * image
        norm_next = jnp.sum(residual * residual)
        direction = residual + norm_next / norm_now * direction
        norm_now = norm_next
    return (solution, residual)
```

```python
import functools

import jax
import jax.numpy as jnp
from jax import lax
from jax.experimental import pallas as pl
from jax.experimental.pallas import tpu as pltpu
from jax.sharding import PartitionSpec as P

TILE = 128
KN = 5
BATCH = 8
HALO = 4
kernel_weight = 0.03125
MESH = pl.DeviceIdType.MESH


def split_rows(value):
    high = value.astype(jnp.bfloat16).astype(jnp.float32)
    return jnp.concatenate([high, value - high], axis=0)


def phi_tile(columns, rows):
    high, rest = [], []
    for start in range(0, TILE, 32):
        square = None
        for axis in range(4, 7):
            gap = columns[start : start + 32, axis : axis + 1] - rows[axis : axis + 1, :]
            square = gap * gap if square is None else square + gap * gap
        ratio = square * lax.rsqrt(jnp.maximum(square, 1e-30))
        margin = jnp.maximum(1.0 - ratio, 0.0)
        twice = margin * margin
        value = twice * twice * (5.0 - 4.0 * margin)
        lead = value.astype(jnp.bfloat16)
        high.append(lead)
        rest.append((value - lead.astype(jnp.float32)).astype(jnp.bfloat16))
    return jnp.concatenate(high + rest, axis=0)


def load_kernel(lists_ref, count_ref, vol_ref, ctrl_ref, load_ref):
    load_ref[...] = jnp.zeros_like(load_ref)
    last = vol_ref.shape[0] - 1

    def step(_, state):
        tile, entry = state
        found = []
        for _ in range(BATCH):
            listed = lists_ref[tile * 8 + entry]
            more = lists_ref[tile * 8 + entry + 1] >= 0
            block = vol_ref[jnp.minimum(tile, last)]
            near = jnp.maximum(listed, 0)
            live = jnp.where(listed >= 0, 1.0, 0.0).astype(jnp.float32)
            kern = phi_tile(block.T, ctrl_ref[near])
            grads = split_rows(block * live).astype(jnp.bfloat16)
            both = jnp.concatenate([grads, grads], axis=1)
            found.append((near, jnp.dot(both, kern, preferred_element_type=jnp.float32)))
            tile, entry = jnp.where(more, tile, tile + 1), jnp.where(more, entry + 1, 0)
        for near, terms in found:
            load_ref[near + HALO] += terms[0:4] + terms[8:12]
        return tile, entry

    lax.fori_loop(0, count_ref[0], step, (jnp.int32(0), jnp.int32(0)))


def solve_kernel(
    vols, ctrls, mask_ref, load_ref, points_ref, sol_ref, res_ref,
    from_pair, to_chip, from_chip, kern, field, first_w, second_w, start_w, sums_a, sums_b,
    pair_send, pair_recv, chip_send, chip_recv, a_send, a_recv, b_send, b_recv,
):
    count = vols * ctrls
    chips = count // 2
    own = sol_ref.shape[0]
    wide = own + 2 * HALO
    vol, ctrl = lax.axis_index("vol"), lax.axis_index("ctrl")
    me = vol * ctrls + ctrl
    chip, core = me // 2, me % 2

    def device(index):
        return {"vol": index // ctrls, "ctrl": index % ctrls}

    barrier = pltpu.get_barrier_semaphore()

    def greet(step, _):
        pl.semaphore_signal(
            barrier, inc=1, device_id=device((me + step) % count), device_id_type=MESH
        )
        return 0

    lax.fori_loop(1, count, greet, 0)
    pl.semaphore_wait(barrier, count - 1)

    def slab(index):
        return pl.ds(index * own, wide)

    def pair_copy(part):
        return pltpu.make_async_remote_copy(
            src_ref=load_ref.at[slab(2 * part + 1 - core)],
            dst_ref=from_pair.at[part],
            send_sem=pair_send.at[part],
            recv_sem=pair_recv.at[part],
            device_id=device(2 * chip + 1 - core),
            device_id_type=MESH,
        )

    def chip_copy(part, slot):
        return pltpu.make_async_remote_copy(
            src_ref=to_chip.at[part],
            dst_ref=from_chip.at[slot],
            send_sem=chip_send.at[part],
            recv_sem=chip_recv.at[slot],
            device_id=device(2 * part + core),
            device_id_type=MESH,
        )

    def start_pair(step, _):
        pair_copy((chip + step) % chips).start()
        return 0

    lax.fori_loop(1, chips + 1, start_pair, 0)

    def forward(step, _):
        part = (chip + step) % chips
        pair_copy(part).wait_recv()
        to_chip[part] = load_ref[slab(2 * part + core)] + from_pair[part]
        chip_copy(part, chip).start()
        return 0

    lax.fori_loop(1, chips, forward, 0)
    pair_copy(chip).wait_recv()
    start_w[...] = load_ref[slab(me)] + from_pair[chip]

    def build(row, _):
        for entry in range(KN):
            away = 1e6 * (1.0 - mask_ref[row * 8 + entry])
            kern[row, entry * 256 : entry * 256 + 256, :] = phi_tile(
                points_ref[row + entry].T, points_ref[row + 2] + away
            )
        return 0

    lax.fori_loop(0, own + HALO, build, 0)

    def gather(step, _):
        part = (chip + step) % chips
        chip_copy(part, part).wait_recv()
        start_w[...] += from_chip[part]
        return 0

    lax.fori_loop(1, chips, gather, 0)

    def spread(source, size):
        def body(row, _):
            parts = split_rows(source[row])
            field[row] = jnp.concatenate([parts, jnp.zeros_like(parts)], axis=0).astype(jnp.bfloat16)
            return 0

        lax.fori_loop(0, size, body, 0)

    def apply(source, target, size, shift):
        spread(source, size + 4)

        def body(step, _):
            mixed = []
            for turn in range(4):
                row = step * 4 + turn
                pieces = []
                for entry in range(KN):
                    pieces += [field[row + entry]] * 2
                mixed.append(
                    jnp.dot(
                        jnp.concatenate(pieces, axis=1),
                        kern[row + shift],
                        preferred_element_type=jnp.float32,
                    )
                )
            for turn in range(4):
                row = step * 4 + turn
                target[row] = source[row + 2] + kernel_weight * (mixed[turn][0:4] + mixed[turn][4:8])
            return 0

        lax.fori_loop(0, size // 4, body, 0)

    def share(sums, send, recv):
        def copy(peer, slot):
            return pltpu.make_async_remote_copy(
                src_ref=sums.at[me],
                dst_ref=sums.at[slot],
                send_sem=send.at[peer],
                recv_sem=recv.at[slot],
                device_id=device(peer),
                device_id_type=MESH,
            )

        def begin(step, _):
            copy((me + step) % count, me).start()
            return 0

        def collect(step, total):
            peer = (me + step) % count
            copy(peer, peer).wait_recv()
            return total + sums[peer]

        def finish(step, _):
            copy((me + step) % count, me).wait_send()
            return 0

        return (
            lambda: lax.fori_loop(1, count, begin, 0),
            lambda: lax.fori_loop(1, count, collect, sums[me]),
            lambda: lax.fori_loop(1, count, finish, 0),
        )

    apply(start_w, first_w, own + 4, 0)
    r0 = start_w[HALO : HALO + own]
    w1 = first_w[2 : 2 + own]
    sums_a[me] = jnp.concatenate([jnp.sum(r0 * r0, axis=0), jnp.sum(r0 * w1, axis=0)], axis=0)
    begin_a, collect_a, finish_a = share(sums_a, a_send, a_recv)
    begin_b, collect_b, finish_b = share(sums_b, b_send, b_recv)
    begin_a()
    apply(first_w, second_w, own, 2)
    total = collect_a()
    rr0, energy0 = jnp.sum(total[0:4]), jnp.sum(total[4:8])
    alpha0 = rr0 / energy0
    r0 = start_w[HALO : HALO + own]
    w1 = first_w[2 : 2 + own]
    r1 = r0 - alpha0 * w1
    image = w1 - alpha0 * second_w[...]
    sums_b[me] = jnp.concatenate(
        [jnp.sum(r1 * r1, axis=0), jnp.sum(r1 * image, axis=0), jnp.sum(r1 * w1, axis=0), jnp.zeros((4, TILE), jnp.float32)],
        axis=0,
    )
    begin_b()
    total = collect_b()
    rr1 = jnp.sum(total[0:4])
    beta = rr1 / rr0
    energy1 = jnp.sum(total[4:8]) + 2.0 * beta * jnp.sum(total[8:12]) + beta * beta * energy0
    alpha1 = rr1 / energy1
    r0 = start_w[HALO : HALO + own]
    w1 = first_w[2 : 2 + own]
    r1 = r0 - alpha0 * w1
    sol_ref[...] = alpha0 * r0 + alpha1 * (r1 + beta * r0)
    res_ref[...] = r1 - alpha1 * (w1 - alpha0 * second_w[...] + beta * w1)

    def drain_pair(part, _):
        pair_copy(part).wait_send()
        return 0

    def drain_chip(step, _):
        chip_copy((chip + step) % chips, chip).wait_send()
        return 0

    lax.fori_loop(0, chips, drain_pair, 0)
    lax.fori_loop(1, chips, drain_chip, 0)
    finish_a()
    finish_b()


def with_neighbours(rows, axes):
    count = lax.axis_size(axes)
    pairs = [(i, i + 1) for i in range(count - 1)]
    before = lax.ppermute(rows[-2:], axes, pairs)
    after = lax.ppermute(rows[:2], axes, [(j, i) for i, j in pairs])
    return jnp.concatenate([before, rows, after], axis=0)


def body(vols, ctrls, ctrl_coords, vol_coords, sensitivity, vol_lists, ctrl_lists):
    f32 = jnp.float32
    axes = ("vol", "ctrl")
    count = vols * ctrls
    tiles = ctrl_coords.shape[1] // TILE
    own = ctrl_lists.shape[0]
    wide = own + 2 * HALO
    vol_tiles = vol_lists.shape[0]
    first = lax.axis_index(axes) * own

    ids = first + jnp.arange(own, dtype=jnp.int32)
    wanted = ids[:, None] + jnp.arange(-2, 3, dtype=jnp.int32)
    listed = jnp.any(ctrl_lists[:, :, None] == wanted[:, None, :], axis=1) & (wanted >= 0)
    mask = with_neighbours(jnp.pad(listed.astype(f32), ((0, 0), (0, 3))), axes).reshape(-1)

    halves = (0.5 * ctrl_coords).reshape(3, tiles, TILE).transpose(1, 0, 2)
    ctrl_pack = jnp.pad(halves, ((0, 0), (4, 1), (0, 0)))
    points = lax.dynamic_slice_in_dim(jnp.pad(ctrl_pack, ((HALO, HALO), (0, 0), (0, 0))), first, wide, 0)
    vol_pack = jnp.concatenate(
        [
            jnp.pad(sensitivity.reshape(3, vol_tiles, TILE), ((0, 1), (0, 0), (0, 0))),
            jnp.pad((0.5 * vol_coords).reshape(3, vol_tiles, TILE), ((0, 1), (0, 0), (0, 0))),
        ],
        axis=0,
    ).transpose(1, 0, 2)
    lists = jnp.pad(vol_lists, ((0, BATCH), (0, 8 - vol_lists.shape[1])), constant_values=-1)
    pairs = jnp.sum(jnp.maximum(jnp.sum((vol_lists >= 0).astype(jnp.int32), axis=1), 1))
    rounds = ((pairs + BATCH - 1) // BATCH).reshape(1)

    vmem = pl.BlockSpec(memory_space=pltpu.VMEM)
    smem = pl.BlockSpec(memory_space=pltpu.SMEM)
    load = pl.pallas_call(
        load_kernel,
        out_shape=jax.ShapeDtypeStruct((tiles + 2 * HALO, 4, TILE), f32),
        in_specs=[smem, smem, vmem, vmem],
        out_specs=vmem,
        compiler_params=pltpu.CompilerParams(vmem_limit_bytes=40 * 2**20),
        name="load_terms",
    )(lists.reshape(-1), rounds, vol_pack, ctrl_pack)

    chips = count // 2
    dma = pltpu.SemaphoreType.DMA
    answer = jax.ShapeDtypeStruct((own, 4, TILE), f32)
    sol, res = pl.pallas_call(
        functools.partial(solve_kernel, vols, ctrls),
        out_shape=(answer, answer),
        in_specs=[smem, vmem, vmem],
        out_specs=(vmem, vmem),
        scratch_shapes=[
            pltpu.VMEM((chips, wide, 4, TILE), f32),
            pltpu.VMEM((chips, wide, 4, TILE), f32),
            pltpu.VMEM((chips, wide, 4, TILE), f32),
            pltpu.VMEM((own + 4, KN * 256, TILE), jnp.bfloat16),
            pltpu.VMEM((wide, 16, TILE), jnp.bfloat16),
            pltpu.VMEM((own + 4, 4, TILE), f32),
            pltpu.VMEM((own, 4, TILE), f32),
            pltpu.VMEM((wide, 4, TILE), f32),
            pltpu.VMEM((count, 8, TILE), f32),
            pltpu.VMEM((count, 16, TILE), f32),
            dma((chips,)), dma((chips,)), dma((chips,)), dma((chips,)),
            dma((count,)), dma((count,)), dma((count,)), dma((count,)),
        ],
        compiler_params=pltpu.CompilerParams(
            collective_id=0, has_side_effects=True, vmem_limit_bytes=40 * 2**20
        ),
        name="scatter_and_solve",
    )(mask, load, points)

    def unpack(value):
        return value.transpose(1, 0, 2)[:3].reshape(3, own * TILE)

    return unpack(sol), unpack(res)


def solution(mesh):
    placed = (
        P(),
        P(None, ("vol", "ctrl")),
        P(None, ("cases", "vol", "ctrl")),
        P(("vol", "ctrl"), None),
        P(("vol", "ctrl"), None),
    )
    return jax.shard_map(
        functools.partial(body, mesh.shape["vol"], mesh.shape["ctrl"]),
        mesh=mesh,
        in_specs=placed,
        out_specs=(P(None, ("cases", "vol", "ctrl")), P(None, ("cases", "vol", "ctrl"))),
        check_vma=False,
    )
```

```python
import functools

import jax
import jax.numpy as jnp
from jax import lax
from jax.experimental import pallas as pl
from jax.experimental.pallas import tpu as pltpu
from jax.sharding import PartitionSpec as P

TILE = 128
KN = 5
BATCH = 16
GROUP = 32
AHEAD = 6
HALO = 4
kernel_weight = 0.03125
MESH = pl.DeviceIdType.MESH


def split_rows(value):
    high = value.astype(jnp.bfloat16).astype(jnp.float32)
    return jnp.concatenate([high, value - high], axis=0)


def phi_tile(columns, rows):
    high, rest = [], []
    for start in range(0, TILE, 32):
        square = None
        for axis in range(3):
            gap = columns(axis, start, 32) - rows[4 + axis : 5 + axis, :]
            square = gap * gap if square is None else square + gap * gap
        ratio = square * lax.rsqrt(jnp.maximum(square, 1e-30))
        margin = jnp.maximum(1.0 - ratio, 0.0)
        twice = margin * margin
        value = twice * twice * (5.0 - 4.0 * margin)
        lead = value.astype(jnp.bfloat16)
        high.append(lead)
        rest.append((value - lead.astype(jnp.float32)).astype(jnp.bfloat16))
    return jnp.concatenate(high + rest, axis=0)


def turn_columns(cols_ref, slot, block):
    for axis in range(3):
        row = block[4 + axis : 5 + axis, :]
        cols_ref[slot, axis] = jnp.broadcast_to(row, (TILE, TILE)).T


def column_reader(cols_ref, slot):
    return lambda axis, start, size: cols_ref[slot, axis, start : start + size, :]


def load_kernel(lists_ref, trips_ref, vol_ref, ctrl_ref, load_ref, cols_even, cols_odd):
    load_ref[...] = jnp.zeros_like(load_ref)
    groups = vol_ref.shape[0] // GROUP

    def fill(slot, _):
        turn_columns(cols_even, slot, vol_ref[slot])
        return 0

    lax.fori_loop(0, GROUP, fill, 0)

    def visit(group, now, later):
        begin = group * GROUP
        end = begin + GROUP
        following = jnp.minimum(group + 1, groups - 1) * GROUP

        def step(index, state):
            tile, entry = state
            for ahead in range(AHEAD):
                slot = jnp.minimum(index * AHEAD + ahead, GROUP - 1)
                turn_columns(later, slot, vol_ref[following + slot])
            found = []
            for _ in range(BATCH):
                inside = tile < end
                mine = jnp.minimum(tile, end - 1)
                listed = lists_ref[mine * 8 + entry]
                more = lists_ref[mine * 8 + entry + 1] >= 0
                near = jnp.maximum(listed, 0)
                live = jnp.where(inside & (listed >= 0), 1.0, 0.0).astype(jnp.float32)
                kern = phi_tile(column_reader(now, mine - begin), ctrl_ref[near])
                grads = split_rows(vol_ref[mine] * live).astype(jnp.bfloat16)
                both = jnp.concatenate([grads, grads], axis=1)
                found.append((near, jnp.dot(both, kern, preferred_element_type=jnp.float32)))
                tile = jnp.where(inside & jnp.logical_not(more), tile + 1, tile)
                entry = jnp.where(inside & more, entry + 1, 0)
            for near, terms in found:
                load_ref[near + HALO] += terms[0:4] + terms[8:12]
            return tile, entry

        lax.fori_loop(0, trips_ref[group], step, (begin, jnp.int32(0)))

    def two(index, _):
        visit(2 * index, cols_even, cols_odd)
        visit(2 * index + 1, cols_odd, cols_even)
        return 0

    lax.fori_loop(0, groups // 2, two, 0)


def solve_kernel(
    vols, ctrls, mask_ref, load_ref, points_ref, sol_ref, res_ref,
    from_pair, to_chip, from_chip, cols, kern, field, first_w, second_w, start_w, sums_a, sums_b,
    pair_send, pair_recv, chip_send, chip_recv, a_send, a_recv, b_send, b_recv,
):
    count = vols * ctrls
    chips = count // 2
    own = sol_ref.shape[0]
    wide = own + 2 * HALO
    vol, ctrl = lax.axis_index("vol"), lax.axis_index("ctrl")
    me = vol * ctrls + ctrl
    chip, core = me // 2, me % 2

    def device(index):
        return {"vol": index // ctrls, "ctrl": index % ctrls}

    barrier = pltpu.get_barrier_semaphore()

    def greet(step, _):
        pl.semaphore_signal(
            barrier, inc=1, device_id=device((me + step) % count), device_id_type=MESH
        )
        return 0

    lax.fori_loop(1, count, greet, 0)
    pl.semaphore_wait(barrier, count - 1)

    def slab(index):
        return pl.ds(index * own, wide)

    def pair_copy(part):
        return pltpu.make_async_remote_copy(
            src_ref=load_ref.at[slab(2 * part + 1 - core)],
            dst_ref=from_pair.at[part],
            send_sem=pair_send.at[part],
            recv_sem=pair_recv.at[part],
            device_id=device(2 * chip + 1 - core),
            device_id_type=MESH,
        )

    def chip_copy(part, slot):
        return pltpu.make_async_remote_copy(
            src_ref=to_chip.at[part],
            dst_ref=from_chip.at[slot],
            send_sem=chip_send.at[part],
            recv_sem=chip_recv.at[slot],
            device_id=device(2 * part + core),
            device_id_type=MESH,
        )

    def start_pair(step, _):
        pair_copy((chip + step) % chips).start()
        return 0

    lax.fori_loop(1, chips + 1, start_pair, 0)

    def forward(step, _):
        part = (chip + step) % chips
        pair_copy(part).wait_recv()
        to_chip[part] = load_ref[slab(2 * part + core)] + from_pair[part]
        chip_copy(part, chip).start()
        return 0

    lax.fori_loop(1, chips, forward, 0)
    pair_copy(chip).wait_recv()
    start_w[...] = load_ref[slab(me)] + from_pair[chip]

    def turn(row, _):
        turn_columns(cols, row, points_ref[row])
        return 0

    lax.fori_loop(0, wide, turn, 0)

    def build(row, _):
        for entry in range(KN):
            away = 1e6 * (1.0 - mask_ref[row * 8 + entry])
            kern[row, entry * 256 : entry * 256 + 256, :] = phi_tile(
                column_reader(cols, row + entry), points_ref[row + 2] + away
            )
        return 0

    lax.fori_loop(0, own + HALO, build, 0)

    def gather(step, _):
        part = (chip + step) % chips
        chip_copy(part, part).wait_recv()
        start_w[...] += from_chip[part]
        return 0

    lax.fori_loop(1, chips, gather, 0)

    def spread(source, size):
        def body(row, _):
            parts = split_rows(source[row])
            field[row] = jnp.concatenate([parts, jnp.zeros_like(parts)], axis=0).astype(jnp.bfloat16)
            return 0

        lax.fori_loop(0, size, body, 0)

    def apply(source, target, size, shift):
        spread(source, size + 4)

        def body(step, _):
            mixed = []
            for turn in range(4):
                row = step * 4 + turn
                pieces = []
                for entry in range(KN):
                    pieces += [field[row + entry]] * 2
                mixed.append(
                    jnp.dot(
                        jnp.concatenate(pieces, axis=1),
                        kern[row + shift],
                        preferred_element_type=jnp.float32,
                    )
                )
            for turn in range(4):
                row = step * 4 + turn
                target[row] = source[row + 2] + kernel_weight * (mixed[turn][0:4] + mixed[turn][4:8])
            return 0

        lax.fori_loop(0, size // 4, body, 0)

    def share(sums, send, recv):
        def copy(peer, slot):
            return pltpu.make_async_remote_copy(
                src_ref=sums.at[me],
                dst_ref=sums.at[slot],
                send_sem=send.at[peer],
                recv_sem=recv.at[slot],
                device_id=device(peer),
                device_id_type=MESH,
            )

        def begin(step, _):
            copy((me + step) % count, me).start()
            return 0

        def collect(step, total):
            peer = (me + step) % count
            copy(peer, peer).wait_recv()
            return total + sums[peer]

        def finish(step, _):
            copy((me + step) % count, me).wait_send()
            return 0

        return (
            lambda: lax.fori_loop(1, count, begin, 0),
            lambda: lax.fori_loop(1, count, collect, sums[me]),
            lambda: lax.fori_loop(1, count, finish, 0),
        )

    apply(start_w, first_w, own + 4, 0)
    r0 = start_w[HALO : HALO + own]
    w1 = first_w[2 : 2 + own]
    sums_a[me] = jnp.concatenate([jnp.sum(r0 * r0, axis=0), jnp.sum(r0 * w1, axis=0)], axis=0)
    begin_a, collect_a, finish_a = share(sums_a, a_send, a_recv)
    begin_b, collect_b, finish_b = share(sums_b, b_send, b_recv)
    begin_a()
    apply(first_w, second_w, own, 2)
    total = collect_a()
    rr0, energy0 = jnp.sum(total[0:4]), jnp.sum(total[4:8])
    alpha0 = rr0 / energy0
    r0 = start_w[HALO : HALO + own]
    w1 = first_w[2 : 2 + own]
    r1 = r0 - alpha0 * w1
    image = w1 - alpha0 * second_w[...]
    sums_b[me] = jnp.concatenate(
        [jnp.sum(r1 * r1, axis=0), jnp.sum(r1 * image, axis=0), jnp.sum(r1 * w1, axis=0), jnp.zeros((4, TILE), jnp.float32)],
        axis=0,
    )
    begin_b()
    total = collect_b()
    rr1 = jnp.sum(total[0:4])
    beta = rr1 / rr0
    energy1 = jnp.sum(total[4:8]) + 2.0 * beta * jnp.sum(total[8:12]) + beta * beta * energy0
    alpha1 = rr1 / energy1
    r0 = start_w[HALO : HALO + own]
    w1 = first_w[2 : 2 + own]
    r1 = r0 - alpha0 * w1
    sol_ref[...] = alpha0 * r0 + alpha1 * (r1 + beta * r0)
    res_ref[...] = r1 - alpha1 * (w1 - alpha0 * second_w[...] + beta * w1)

    def drain_pair(part, _):
        pair_copy(part).wait_send()
        return 0

    def drain_chip(step, _):
        chip_copy((chip + step) % chips, chip).wait_send()
        return 0

    lax.fori_loop(0, chips, drain_pair, 0)
    lax.fori_loop(1, chips, drain_chip, 0)
    finish_a()
    finish_b()


def with_neighbours(rows, axes):
    count = lax.axis_size(axes)
    pairs = [(i, i + 1) for i in range(count - 1)]
    before = lax.ppermute(rows[-2:], axes, pairs)
    after = lax.ppermute(rows[:2], axes, [(j, i) for i, j in pairs])
    return jnp.concatenate([before, rows, after], axis=0)


def body(vols, ctrls, ctrl_coords, vol_coords, sensitivity, vol_lists, ctrl_lists):
    f32 = jnp.float32
    axes = ("vol", "ctrl")
    count = vols * ctrls
    tiles = ctrl_coords.shape[1] // TILE
    own = ctrl_lists.shape[0]
    wide = own + 2 * HALO
    vol_tiles = vol_lists.shape[0]
    first = lax.axis_index(axes) * own

    ids = first + jnp.arange(own, dtype=jnp.int32)
    wanted = ids[:, None] + jnp.arange(-2, 3, dtype=jnp.int32)
    listed = jnp.any(ctrl_lists[:, :, None] == wanted[:, None, :], axis=1) & (wanted >= 0)
    mask = with_neighbours(jnp.pad(listed.astype(f32), ((0, 0), (0, 3))), axes).reshape(-1)

    halves = (0.5 * ctrl_coords).reshape(3, tiles, TILE).transpose(1, 0, 2)
    ctrl_pack = jnp.pad(halves, ((0, 0), (4, 1), (0, 0)))
    points = lax.dynamic_slice_in_dim(jnp.pad(ctrl_pack, ((HALO, HALO), (0, 0), (0, 0))), first, wide, 0)
    vol_pack = jnp.concatenate(
        [
            jnp.pad(sensitivity.reshape(3, vol_tiles, TILE), ((0, 1), (0, 0), (0, 0))),
            jnp.pad((0.5 * vol_coords).reshape(3, vol_tiles, TILE), ((0, 1), (0, 0), (0, 0))),
        ],
        axis=0,
    ).transpose(1, 0, 2)
    lists = jnp.pad(vol_lists, ((0, 0), (0, 8 - vol_lists.shape[1])), constant_values=-1)
    pairs = jnp.maximum(jnp.sum((vol_lists >= 0).astype(jnp.int32), axis=1), 1)
    trips = (jnp.sum(pairs.reshape(-1, GROUP), axis=1) + BATCH - 1) // BATCH
    trips = jnp.maximum(trips, -(-GROUP // AHEAD))

    vmem = pl.BlockSpec(memory_space=pltpu.VMEM)
    smem = pl.BlockSpec(memory_space=pltpu.SMEM)
    load = pl.pallas_call(
        load_kernel,
        out_shape=jax.ShapeDtypeStruct((tiles + 2 * HALO, 4, TILE), f32),
        in_specs=[smem, smem, vmem, vmem],
        out_specs=vmem,
        scratch_shapes=[pltpu.VMEM((GROUP, 3, TILE, TILE), f32)] * 2,
        compiler_params=pltpu.CompilerParams(vmem_limit_bytes=40 * 2**20),
        name="load_terms",
    )(lists.reshape(-1), trips, vol_pack, ctrl_pack)

    chips = count // 2
    dma = pltpu.SemaphoreType.DMA
    answer = jax.ShapeDtypeStruct((own, 4, TILE), f32)
    sol, res = pl.pallas_call(
        functools.partial(solve_kernel, vols, ctrls),
        out_shape=(answer, answer),
        in_specs=[smem, vmem, vmem],
        out_specs=(vmem, vmem),
        scratch_shapes=[
            pltpu.VMEM((chips, wide, 4, TILE), f32),
            pltpu.VMEM((chips, wide, 4, TILE), f32),
            pltpu.VMEM((chips, wide, 4, TILE), f32),
            pltpu.VMEM((wide, 3, TILE, TILE), f32),
            pltpu.VMEM((own + 4, KN * 256, TILE), jnp.bfloat16),
            pltpu.VMEM((wide, 16, TILE), jnp.bfloat16),
            pltpu.VMEM((own + 4, 4, TILE), f32),
            pltpu.VMEM((own, 4, TILE), f32),
            pltpu.VMEM((wide, 4, TILE), f32),
            pltpu.VMEM((count, 8, TILE), f32),
            pltpu.VMEM((count, 16, TILE), f32),
            dma((chips,)), dma((chips,)), dma((chips,)), dma((chips,)),
            dma((count,)), dma((count,)), dma((count,)), dma((count,)),
        ],
        compiler_params=pltpu.CompilerParams(
            collective_id=0, has_side_effects=True, vmem_limit_bytes=40 * 2**20
        ),
        name="scatter_and_solve",
    )(mask, load, points)

    def unpack(value):
        return value.transpose(1, 0, 2)[:3].reshape(3, own * TILE)

    return unpack(sol), unpack(res)


def solution(mesh):
    placed = (
        P(),
        P(None, ("vol", "ctrl")),
        P(None, ("cases", "vol", "ctrl")),
        P(("vol", "ctrl"), None),
        P(("vol", "ctrl"), None),
    )
    return jax.shard_map(
        functools.partial(body, mesh.shape["vol"], mesh.shape["ctrl"]),
        mesh=mesh,
        in_specs=placed,
        out_specs=(P(None, ("cases", "vol", "ctrl")), P(None, ("cases", "vol", "ctrl"))),
        check_vma=False,
    )
```

```python
import functools

import jax
import jax.numpy as jnp
from jax import lax
from jax.experimental import pallas as pl
from jax.experimental.pallas import tpu as pltpu
from jax.sharding import PartitionSpec as P

TILE = 128
KN = 5
BATCH = 16
GROUP = 32
AHEAD = 6
HALO = 4
kernel_weight = 0.03125
MESH = pl.DeviceIdType.MESH


def split_rows(value):
    high = value.astype(jnp.bfloat16).astype(jnp.float32)
    return jnp.concatenate([high, value - high], axis=0)


def phi_tile(columns, rows):
    high, rest = [], []
    for start in range(0, TILE, 32):
        square = None
        for axis in range(3):
            gap = columns(axis, start, 32) - rows[4 + axis : 5 + axis, :]
            square = gap * gap if square is None else square + gap * gap
        ratio = square * lax.rsqrt(jnp.maximum(square, 1e-30))
        margin = jnp.maximum(4.0 - ratio, 0.0)
        twice = margin * margin
        value = twice * twice * (5.0 - margin)
        lead = value.astype(jnp.bfloat16)
        high.append(lead)
        rest.append((value - lead.astype(jnp.float32)).astype(jnp.bfloat16))
    return jnp.concatenate(high + rest, axis=0)


def turn_columns(cols_ref, slot, block):
    for axis in range(3):
        row = block[4 + axis : 5 + axis, :]
        cols_ref[slot, axis] = jnp.broadcast_to(row, (TILE, TILE)).T


def column_reader(cols_ref, slot):
    return lambda axis, start, size: cols_ref[slot, axis, start : start + size, :]


def load_kernel(
    own, half, lists_ref, order_ref, trips_ref, grads_ref, points_ref, ctrl_ref, load_ref, cols_even, cols_odd
):
    load_ref[...] = jnp.zeros_like(load_ref)
    groups = points_ref.shape[0] // GROUP
    active = trips_ref[groups]

    def fill(slot, _):
        turn_columns(cols_even, slot, points_ref[order_ref[slot]])
        return 0

    lax.fori_loop(0, GROUP, fill, 0)

    def visit(group, now, later):
        begin = group * GROUP
        end = jnp.minimum(begin + GROUP, active)
        following = jnp.minimum(group + 1, groups - 1) * GROUP

        def step(index, state):
            tile, entry = state
            for ahead in range(AHEAD):
                slot = jnp.minimum(index * AHEAD + ahead, GROUP - 1)
                turn_columns(later, slot, points_ref[order_ref[following + slot]])
            found = []
            for _ in range(BATCH):
                inside = tile < end
                mine = jnp.maximum(jnp.minimum(tile, end - 1), begin)
                real = order_ref[mine]
                listed = lists_ref[real * 8 + entry]
                more = lists_ref[real * 8 + entry + 1] >= 0
                near = jnp.maximum(listed, 0)
                live = jnp.where(inside & (listed >= 0), 1.0 / 256.0, 0.0).astype(jnp.float32)
                kern = phi_tile(column_reader(now, mine - begin), ctrl_ref[near])
                grads = split_rows(grads_ref[real] * live).astype(jnp.bfloat16)
                both = jnp.concatenate([grads, grads], axis=1)
                place = lax.div(near, own) * half + lax.rem(near, half) + HALO
                found.append((place, jnp.dot(both, kern, preferred_element_type=jnp.float32)))
                tile = jnp.where(inside & jnp.logical_not(more), tile + 1, tile)
                entry = jnp.where(inside & more, entry + 1, 0)
            for place, terms in found:
                load_ref[place] += terms[0:8] + terms[8:16]
            return tile, entry

        lax.fori_loop(0, trips_ref[group], step, (begin, jnp.int32(0)))

    def two(index, _):
        visit(2 * index, cols_even, cols_odd)
        visit(2 * index + 1, cols_odd, cols_even)
        return 0

    lax.fori_loop(0, groups // 2, two, 0)


def solve_kernel(
    vols, ctrls, shared, mask_ref, load_ref, points_ref, sol_ref, res_ref,
    from_pair, to_chip, from_chip, gathered, to_case, parts, cols, kern, field, first_w, second_w, start_w, sums_a, sums_b,
    pair_send, pair_recv, chip_send, chip_recv, a_send, a_recv, b_send, b_recv, case_send, case_recv,
):
    count = vols * ctrls
    chips = count // 2
    own = sol_ref.shape[0]
    wide = own + 2 * HALO
    vol, ctrl = lax.axis_index("vol"), lax.axis_index("ctrl")
    me = vol * ctrls + ctrl
    chip, core = me // 2, me % 2
    case = lax.axis_index("cases")
    half = own // 2 if shared else own
    width = gathered.shape[0]

    def device(index):
        return {"vol": index // ctrls, "ctrl": index % ctrls}

    barrier = pltpu.get_barrier_semaphore()

    def greet(step, _):
        pl.semaphore_signal(
            barrier, inc=1, device_id=device((me + step) % count), device_id_type=MESH
        )
        return 0

    lax.fori_loop(1, count, greet, 0)
    if shared:
        pl.semaphore_signal(barrier, inc=1, device_id={"cases": 1 - case}, device_id_type=MESH)
    pl.semaphore_wait(barrier, count if shared else count - 1)

    def slab(index):
        return pl.ds(index * half + (HALO - HALO * case if shared else 0), width)

    def pair_copy(part):
        return pltpu.make_async_remote_copy(
            src_ref=load_ref.at[slab(2 * part + 1 - core)],
            dst_ref=from_pair.at[part],
            send_sem=pair_send.at[part],
            recv_sem=pair_recv.at[part],
            device_id=device(2 * chip + 1 - core),
            device_id_type=MESH,
        )

    def chip_copy(part, slot):
        return pltpu.make_async_remote_copy(
            src_ref=to_chip.at[part],
            dst_ref=from_chip.at[slot],
            send_sem=chip_send.at[part],
            recv_sem=chip_recv.at[slot],
            device_id=device(2 * part + core),
            device_id_type=MESH,
        )

    def start_pair(step, _):
        pair_copy((chip + step) % chips).start()
        return 0

    lax.fori_loop(1, chips + 1, start_pair, 0)

    def forward(step, _):
        part = (chip + step) % chips
        pair_copy(part).wait_recv()
        to_chip[part] = load_ref[slab(2 * part + core)] + from_pair[part]
        chip_copy(part, chip).start()
        return 0

    lax.fori_loop(1, chips, forward, 0)
    pair_copy(chip).wait_recv()
    gathered[...] = load_ref[slab(me)] + from_pair[chip]

    def turn(row, _):
        turn_columns(cols, row, points_ref[row])
        return 0

    lax.fori_loop(0, wide, turn, 0)

    def build(row, _):
        for entry in range(KN):
            away = 1e6 * (1.0 - mask_ref[row * 8 + entry])
            kern[row, entry * 256 : entry * 256 + 256, :] = phi_tile(
                column_reader(cols, row + entry), points_ref[row + 2] + away
            )
        return 0

    lax.fori_loop(0, own + HALO, build, 0)

    def gather(step, _):
        part = (chip + step) % chips
        chip_copy(part, part).wait_recv()
        gathered[...] += from_chip[part]
        return 0

    lax.fori_loop(1, chips, gather, 0)

    if shared:
        parts[case] = gathered[:, 0:4]
        to_case[...] = gathered[:, 4:8]
        swap = pltpu.make_async_remote_copy(
            src_ref=to_case,
            dst_ref=parts.at[case],
            send_sem=case_send.at[0],
            recv_sem=case_recv.at[0],
            device_id={"cases": 1 - case},
            device_id_type=MESH,
        )
        swap.start()
        swap.wait()
        start_w[HALO : HALO + half] = parts[0, 0:half]
        start_w[HALO + own : wide] = parts[0, half:width]
        start_w[0:HALO] = parts[1, 0:HALO]
        start_w[HALO + half : HALO + own] = parts[1, HALO:width]
    else:
        start_w[...] = gathered[:, 0:4]

    def spread(source, size):
        def body(row, _):
            parts = split_rows(source[row])
            field[row] = jnp.concatenate([parts, jnp.zeros_like(parts)], axis=0).astype(jnp.bfloat16)
            return 0

        lax.fori_loop(0, size, body, 0)

    def apply(source, target, size, shift):
        spread(source, size + 4)

        def body(step, _):
            mixed = []
            for turn in range(4):
                row = step * 4 + turn
                pieces = []
                for entry in range(KN):
                    pieces += [field[row + entry]] * 2
                mixed.append(
                    jnp.dot(
                        jnp.concatenate(pieces, axis=1),
                        kern[row + shift],
                        preferred_element_type=jnp.float32,
                    )
                )
            for turn in range(4):
                row = step * 4 + turn
                target[row] = source[row + 2] + kernel_weight / 256.0 * (mixed[turn][0:4] + mixed[turn][4:8])
            return 0

        lax.fori_loop(0, size // 4, body, 0)

    def share(sums, send, recv):
        def copy(peer, slot):
            return pltpu.make_async_remote_copy(
                src_ref=sums.at[me],
                dst_ref=sums.at[slot],
                send_sem=send.at[peer],
                recv_sem=recv.at[slot],
                device_id=device(peer),
                device_id_type=MESH,
            )

        def begin(step, _):
            copy((me + step) % count, me).start()
            return 0

        def collect(step, total):
            peer = (me + step) % count
            copy(peer, peer).wait_recv()
            return total + sums[peer]

        def finish(step, _):
            copy((me + step) % count, me).wait_send()
            return 0

        return (
            lambda: lax.fori_loop(1, count, begin, 0),
            lambda: lax.fori_loop(1, count, collect, sums[me]),
            lambda: lax.fori_loop(1, count, finish, 0),
        )

    apply(start_w, first_w, own + 4, 0)
    r0 = start_w[HALO : HALO + own]
    w1 = first_w[2 : 2 + own]
    sums_a[me] = jnp.concatenate([jnp.sum(r0 * r0, axis=0), jnp.sum(r0 * w1, axis=0)], axis=0)
    begin_a, collect_a, finish_a = share(sums_a, a_send, a_recv)
    begin_b, collect_b, finish_b = share(sums_b, b_send, b_recv)
    begin_a()
    apply(first_w, second_w, own, 2)
    total = collect_a()
    rr0, energy0 = jnp.sum(total[0:4]), jnp.sum(total[4:8])
    alpha0 = rr0 / energy0
    r0 = start_w[HALO : HALO + own]
    w1 = first_w[2 : 2 + own]
    r1 = r0 - alpha0 * w1
    image = w1 - alpha0 * second_w[...]
    sums_b[me] = jnp.concatenate(
        [jnp.sum(r1 * r1, axis=0), jnp.sum(r1 * image, axis=0), jnp.sum(r1 * w1, axis=0), jnp.zeros((4, TILE), jnp.float32)],
        axis=0,
    )
    begin_b()
    total = collect_b()
    rr1 = jnp.sum(total[0:4])
    beta = rr1 / rr0
    energy1 = jnp.sum(total[4:8]) + 2.0 * beta * jnp.sum(total[8:12]) + beta * beta * energy0
    alpha1 = rr1 / energy1
    r0 = start_w[HALO : HALO + own]
    w1 = first_w[2 : 2 + own]
    r1 = r0 - alpha0 * w1
    sol_ref[...] = alpha0 * r0 + alpha1 * (r1 + beta * r0)
    res_ref[...] = r1 - alpha1 * (w1 - alpha0 * second_w[...] + beta * w1)

    def drain_pair(part, _):
        pair_copy(part).wait_send()
        return 0

    def drain_chip(step, _):
        chip_copy((chip + step) % chips, chip).wait_send()
        return 0

    lax.fori_loop(0, chips, drain_pair, 0)
    lax.fori_loop(1, chips, drain_chip, 0)
    finish_a()
    finish_b()


def with_neighbours(rows, axes):
    count = lax.axis_size(axes)
    pairs = [(i, i + 1) for i in range(count - 1)]
    before = lax.ppermute(rows[-2:], axes, pairs)
    after = lax.ppermute(rows[:2], axes, [(j, i) for i, j in pairs])
    return jnp.concatenate([before, rows, after], axis=0)


def body(vols, ctrls, ctrl_coords, vol_coords, sensitivity, vol_lists, ctrl_lists):
    f32 = jnp.float32
    axes = ("vol", "ctrl")
    count = vols * ctrls
    tiles = ctrl_coords.shape[1] // TILE
    own = ctrl_lists.shape[0]
    wide = own + 2 * HALO
    vol_tiles = vol_lists.shape[0]
    first = lax.axis_index(axes) * own

    ids = first + jnp.arange(own, dtype=jnp.int32)
    wanted = ids[:, None] + jnp.arange(-2, 3, dtype=jnp.int32)
    listed = jnp.any(ctrl_lists[:, :, None] == wanted[:, None, :], axis=1) & (wanted >= 0)
    mask = with_neighbours(jnp.pad(listed.astype(f32), ((0, 0), (0, 3))), axes).reshape(-1)

    doubles = (2.0 * ctrl_coords).reshape(3, tiles, TILE).transpose(1, 0, 2)
    ctrl_pack = jnp.pad(doubles, ((0, 0), (4, 1), (0, 0)))
    points = lax.dynamic_slice_in_dim(jnp.pad(ctrl_pack, ((HALO, HALO), (0, 0), (0, 0))), first, wide, 0)
    vol_pack = jnp.pad((2.0 * vol_coords).reshape(3, vol_tiles, TILE).transpose(1, 0, 2), ((0, 0), (4, 1), (0, 0)))

    shared = lax.axis_size("cases") == 2 and own % 2 == 0 and own // 2 >= HALO
    half = own // 2 if shared else own
    width = half + HALO if shared else wide
    if shared:
        other = lax.ppermute(sensitivity, "cases", [(0, 1), (1, 0)])
        live = (vol_lists >= 0) & (vol_lists // half % 2 == lax.axis_index("cases"))
    else:
        other = jnp.zeros_like(sensitivity)
        live = vol_lists >= 0

    def by_tile(value):
        return jnp.pad(value.reshape(3, vol_tiles, TILE), ((0, 1), (0, 0), (0, 0)))

    grads = jnp.concatenate([by_tile(sensitivity), by_tile(other)], axis=0).transpose(1, 0, 2)
    rank = jnp.cumsum(live.astype(jnp.int32), axis=1) - 1
    slots = jnp.arange(8, dtype=jnp.int32)
    chosen = live[:, :, None] & (rank[:, :, None] == slots)
    lists = jnp.sum(jnp.where(chosen, vol_lists[:, :, None] + 1, 0), axis=1) - 1
    pairs = jnp.sum(live.astype(jnp.int32), axis=1)
    place = jnp.cumsum((pairs > 0).astype(jnp.int32)) - 1
    active = place[-1] + 1
    at = jnp.arange(vol_tiles, dtype=jnp.int32)
    taken = (place[None, :] == at[:, None]) & (pairs > 0)[None, :]
    order = jnp.sum(jnp.where(taken, at[None, :], 0), axis=1)
    sizes = jnp.sum(jnp.where(taken, pairs[None, :], 0), axis=1)
    batches = (jnp.sum(sizes.reshape(-1, GROUP), axis=1) + BATCH - 1) // BATCH
    trips = jnp.where(batches > 0, jnp.maximum(batches, -(-GROUP // AHEAD)), 0)
    trips = jnp.concatenate([trips, active[None]])

    vmem = pl.BlockSpec(memory_space=pltpu.VMEM)
    smem = pl.BlockSpec(memory_space=pltpu.SMEM)
    load_tiles = tiles // own * half + 2 * HALO
    load = pl.pallas_call(
        functools.partial(load_kernel, own, half),
        out_shape=jax.ShapeDtypeStruct((load_tiles, 8, TILE), f32),
        in_specs=[smem, smem, smem, vmem, vmem, vmem],
        out_specs=vmem,
        scratch_shapes=[pltpu.VMEM((GROUP, 3, TILE, TILE), f32)] * 2,
        compiler_params=pltpu.CompilerParams(vmem_limit_bytes=40 * 2**20),
        name="load_terms",
    )(lists.reshape(-1), order, trips, grads, vol_pack, ctrl_pack)

    chips = count // 2
    dma = pltpu.SemaphoreType.DMA
    answer = jax.ShapeDtypeStruct((own, 4, TILE), f32)
    sol, res = pl.pallas_call(
        functools.partial(solve_kernel, vols, ctrls, shared),
        out_shape=(answer, answer),
        in_specs=[smem, vmem, vmem],
        out_specs=(vmem, vmem),
        scratch_shapes=[
            pltpu.VMEM((chips, width, 8, TILE), f32),
            pltpu.VMEM((chips, width, 8, TILE), f32),
            pltpu.VMEM((chips, width, 8, TILE), f32),
            pltpu.VMEM((width, 8, TILE), f32),
            pltpu.VMEM((width, 4, TILE), f32),
            pltpu.VMEM((2, width, 4, TILE), f32),
            pltpu.VMEM((wide, 3, TILE, TILE), f32),
            pltpu.VMEM((own + 4, KN * 256, TILE), jnp.bfloat16),
            pltpu.VMEM((wide, 16, TILE), jnp.bfloat16),
            pltpu.VMEM((own + 4, 4, TILE), f32),
            pltpu.VMEM((own, 4, TILE), f32),
            pltpu.VMEM((wide, 4, TILE), f32),
            pltpu.VMEM((count, 8, TILE), f32),
            pltpu.VMEM((count, 16, TILE), f32),
            dma((chips,)), dma((chips,)), dma((chips,)), dma((chips,)),
            dma((count,)), dma((count,)), dma((count,)), dma((count,)), dma((1,)), dma((1,)),
        ],
        compiler_params=pltpu.CompilerParams(
            collective_id=0, has_side_effects=True, vmem_limit_bytes=40 * 2**20
        ),
        name="scatter_and_solve",
    )(mask, load, points)

    def unpack(value):
        return value.transpose(1, 0, 2)[:3].reshape(3, own * TILE)

    return unpack(sol), unpack(res)


def solution(mesh):
    placed = (
        P(),
        P(None, ("vol", "ctrl")),
        P(None, ("cases", "vol", "ctrl")),
        P(("vol", "ctrl"), None),
        P(("vol", "ctrl"), None),
    )
    return jax.shard_map(
        functools.partial(body, mesh.shape["vol"], mesh.shape["ctrl"]),
        mesh=mesh,
        in_specs=placed,
        out_specs=(P(None, ("cases", "vol", "ctrl")), P(None, ("cases", "vol", "ctrl"))),
        check_vma=False,
    )
```

```python
import functools

import jax
import jax.numpy as jnp
from jax import lax
from jax.experimental import pallas as pl
from jax.experimental.pallas import tpu as pltpu
from jax.sharding import PartitionSpec as P

TILE = 128
KN = 5
BATCH = 16
GROUP = 32
AHEAD = 6
HALO = 4
kernel_weight = 0.03125
MESH = pl.DeviceIdType.MESH


def split_rows(value):
    high = value.astype(jnp.bfloat16).astype(jnp.float32)
    return jnp.concatenate([high, value - high], axis=0)


def phi_tile(columns, rows):
    high, rest = [], []
    for start in range(0, TILE, 32):
        square = None
        for axis in range(3):
            gap = columns(axis, start, 32) - rows[4 + axis : 5 + axis, :]
            square = gap * gap if square is None else square + gap * gap
        ratio = square * lax.rsqrt(jnp.maximum(square, 1e-30))
        margin = jnp.maximum(4.0 - ratio, 0.0)
        twice = margin * margin
        value = twice * twice * (5.0 - margin)
        lead = value.astype(jnp.bfloat16)
        high.append(lead)
        rest.append((value - lead.astype(jnp.float32)).astype(jnp.bfloat16))
    return jnp.concatenate(high + rest, axis=0)


def turn_columns(cols_ref, slot, block):
    for axis in range(3):
        row = block[4 + axis : 5 + axis, :]
        cols_ref[slot, axis] = jnp.broadcast_to(row, (TILE, TILE)).T


def column_reader(cols_ref, slot):
    return lambda axis, start, size: cols_ref[slot, axis, start : start + size, :]


def load_kernel(
    own, half, lists_ref, order_ref, trips_ref, grads_ref, points_ref, ctrl_ref, load_ref, cols_even, cols_odd
):
    load_ref[...] = jnp.zeros_like(load_ref)
    groups = points_ref.shape[0] // GROUP
    active = trips_ref[groups]

    def fill(slot, _):
        turn_columns(cols_even, slot, points_ref[order_ref[slot]])
        return 0

    lax.fori_loop(0, GROUP, fill, 0)

    def visit(group, now, later):
        begin = group * GROUP
        end = jnp.minimum(begin + GROUP, active)
        following = jnp.minimum(group + 1, groups - 1) * GROUP

        def step(index, state):
            tile, entry = state
            for ahead in range(AHEAD):
                slot = jnp.minimum(index * AHEAD + ahead, GROUP - 1)
                turn_columns(later, slot, points_ref[order_ref[following + slot]])
            found = []
            for _ in range(BATCH):
                inside = tile < end
                mine = jnp.maximum(jnp.minimum(tile, end - 1), begin)
                real = order_ref[mine]
                listed = lists_ref[real * 8 + entry]
                more = lists_ref[real * 8 + entry + 1] >= 0
                near = jnp.maximum(listed, 0)
                live = jnp.where(inside & (listed >= 0), 1.0 / 256.0, 0.0).astype(jnp.float32)
                kern = phi_tile(column_reader(now, mine - begin), ctrl_ref[near])
                grads = split_rows(grads_ref[real] * live).astype(jnp.bfloat16)
                both = jnp.concatenate([grads, grads], axis=1)
                place = lax.div(near, own) * half + lax.rem(near, half) + HALO
                found.append((place, jnp.dot(both, kern, preferred_element_type=jnp.float32)))
                tile = jnp.where(inside & jnp.logical_not(more), tile + 1, tile)
                entry = jnp.where(inside & more, entry + 1, 0)
            for place, terms in found:
                load_ref[place] += terms[0:8] + terms[8:16]
            return tile, entry

        lax.fori_loop(0, trips_ref[group], step, (begin, jnp.int32(0)))

    def two(index, _):
        visit(2 * index, cols_even, cols_odd)
        visit(2 * index + 1, cols_odd, cols_even)
        return 0

    lax.fori_loop(0, groups // 2, two, 0)


def solve_kernel(
    vols, ctrls, shared, mask_ref, load_ref, points_ref, sol_ref, res_ref,
    from_pair, to_chip, from_chip, gathered, to_case, parts, away, cols, kern, field, first_w, second_w, start_w, sums_a, sums_b,
    pair_send, pair_recv, chip_send, chip_recv, a_send, a_recv, b_send, b_recv, case_send, case_recv, edge_send, edge_recv,
):
    count = vols * ctrls
    chips = count // 2
    own = sol_ref.shape[0]
    wide = own + 2 * HALO
    vol, ctrl = lax.axis_index("vol"), lax.axis_index("ctrl")
    me = vol * ctrls + ctrl
    chip, core = me // 2, me % 2
    case = lax.axis_index("cases")
    half = own // 2 if shared else own
    width = gathered.shape[0]

    def device(index):
        return {"vol": index // ctrls, "ctrl": index % ctrls}

    barrier = pltpu.get_barrier_semaphore()

    def greet(step, _):
        pl.semaphore_signal(
            barrier, inc=1, device_id=device((me + step) % count), device_id_type=MESH
        )
        return 0

    lax.fori_loop(1, count, greet, 0)
    if shared:
        pl.semaphore_signal(barrier, inc=1, device_id={"cases": 1 - case}, device_id_type=MESH)
    pl.semaphore_wait(barrier, count if shared else count - 1)

    def slab(index):
        return pl.ds(index * half + (HALO - HALO * case if shared else 0), width)

    def pair_copy(part):
        return pltpu.make_async_remote_copy(
            src_ref=load_ref.at[slab(2 * part + 1 - core)],
            dst_ref=from_pair.at[part],
            send_sem=pair_send.at[part],
            recv_sem=pair_recv.at[part],
            device_id=device(2 * chip + 1 - core),
            device_id_type=MESH,
        )

    def chip_copy(part, slot):
        return pltpu.make_async_remote_copy(
            src_ref=to_chip.at[part],
            dst_ref=from_chip.at[slot],
            send_sem=chip_send.at[part],
            recv_sem=chip_recv.at[slot],
            device_id=device(2 * part + core),
            device_id_type=MESH,
        )

    def edge_copy(side):
        return pltpu.make_async_remote_copy(
            src_ref=mask_ref.at[pl.ds((0, own - 2)[side], 2)],
            dst_ref=away.at[pl.ds((own + 2, 0)[side], 2)],
            send_sem=edge_send.at[side],
            recv_sem=edge_recv.at[side],
            device_id=device((me + (count - 1, 1)[side]) % count),
            device_id_type=MESH,
        )

    for side in range(2):
        edge_copy(side).start()
    away[2 : 2 + own] = mask_ref[...]

    def start_pair(step, _):
        pair_copy((chip + step) % chips).start()
        return 0

    lax.fori_loop(1, chips + 1, start_pair, 0)

    def forward(step, _):
        part = (chip + step) % chips
        pair_copy(part).wait_recv()
        to_chip[part] = load_ref[slab(2 * part + core)] + from_pair[part]
        chip_copy(part, chip).start()
        return 0

    lax.fori_loop(1, chips, forward, 0)
    pair_copy(chip).wait_recv()
    gathered[...] = load_ref[slab(me)] + from_pair[chip]

    def turn(row, _):
        turn_columns(cols, row, points_ref[row])
        return 0

    lax.fori_loop(0, wide, turn, 0)

    for side in range(2):
        edge_copy(side).wait()

    def build(row, _):
        for entry in range(KN):
            kern[row, entry * 256 : entry * 256 + 256, :] = phi_tile(
                column_reader(cols, row + entry), points_ref[row + 2] + away[row, entry : entry + 1, :]
            )
        return 0

    lax.fori_loop(0, own + HALO, build, 0)

    def gather(step, _):
        part = (chip + step) % chips
        chip_copy(part, part).wait_recv()
        gathered[...] += from_chip[part]
        return 0

    lax.fori_loop(1, chips, gather, 0)

    if shared:
        parts[case] = gathered[:, 0:4]
        to_case[...] = gathered[:, 4:8]
        swap = pltpu.make_async_remote_copy(
            src_ref=to_case,
            dst_ref=parts.at[case],
            send_sem=case_send.at[0],
            recv_sem=case_recv.at[0],
            device_id={"cases": 1 - case},
            device_id_type=MESH,
        )
        swap.start()
        swap.wait()
        start_w[HALO : HALO + half] = parts[0, 0:half]
        start_w[HALO + own : wide] = parts[0, half:width]
        start_w[0:HALO] = parts[1, 0:HALO]
        start_w[HALO + half : HALO + own] = parts[1, HALO:width]
    else:
        start_w[...] = gathered[:, 0:4]

    def spread(source, size):
        value = source[0:size]
        lead = value.astype(jnp.bfloat16).astype(jnp.float32)
        blank = jnp.zeros((size, 8, TILE), jnp.float32)
        field[0:size] = jnp.concatenate([lead, value - lead, blank], axis=1).astype(jnp.bfloat16)

    def apply(source, target, size, shift):
        spread(source, size + 4)
        many = next(k for k in (12, 8, 4) if size % k == 0)

        def body(step, _):
            mixed = []
            for turn in range(many):
                row = step * many + turn
                pieces = []
                for entry in range(KN):
                    pieces += [field[row + entry]] * 2
                mixed.append(
                    jnp.dot(
                        jnp.concatenate(pieces, axis=1),
                        kern[row + shift],
                        preferred_element_type=jnp.float32,
                    )
                )
            for turn in range(many):
                row = step * many + turn
                target[row] = source[row + 2] + kernel_weight / 256.0 * (mixed[turn][0:4] + mixed[turn][4:8])
            return 0

        lax.fori_loop(0, size // many, body, 0)

    def share(sums, send, recv):
        def copy(peer, slot):
            return pltpu.make_async_remote_copy(
                src_ref=sums.at[me],
                dst_ref=sums.at[slot],
                send_sem=send.at[peer],
                recv_sem=recv.at[slot],
                device_id=device(peer),
                device_id_type=MESH,
            )

        def begin(step, _):
            copy((me + step) % count, me).start()
            return 0

        def collect(step, total):
            peer = (me + step) % count
            copy(peer, peer).wait_recv()
            return total + sums[peer]

        def finish(step, _):
            copy((me + step) % count, me).wait_send()
            return 0

        return (
            lambda: lax.fori_loop(1, count, begin, 0),
            lambda: lax.fori_loop(1, count, collect, sums[me]),
            lambda: lax.fori_loop(1, count, finish, 0),
        )

    apply(start_w, first_w, own + 4, 0)
    r0 = start_w[HALO : HALO + own]
    w1 = first_w[2 : 2 + own]
    sums_a[me] = jnp.concatenate([jnp.sum(r0 * r0, axis=0), jnp.sum(r0 * w1, axis=0)], axis=0)
    begin_a, collect_a, finish_a = share(sums_a, a_send, a_recv)
    begin_b, collect_b, finish_b = share(sums_b, b_send, b_recv)
    begin_a()
    apply(first_w, second_w, own, 2)
    total = collect_a()
    rr0, energy0 = jnp.sum(total[0:4]), jnp.sum(total[4:8])
    alpha0 = rr0 / energy0
    r0 = start_w[HALO : HALO + own]
    w1 = first_w[2 : 2 + own]
    r1 = r0 - alpha0 * w1
    image = w1 - alpha0 * second_w[...]
    sums_b[me] = jnp.concatenate(
        [jnp.sum(r1 * r1, axis=0), jnp.sum(r1 * image, axis=0), jnp.sum(r1 * w1, axis=0), jnp.zeros((4, TILE), jnp.float32)],
        axis=0,
    )
    begin_b()
    total = collect_b()
    rr1 = jnp.sum(total[0:4])
    beta = rr1 / rr0
    energy1 = jnp.sum(total[4:8]) + 2.0 * beta * jnp.sum(total[8:12]) + beta * beta * energy0
    alpha1 = rr1 / energy1
    r0 = start_w[HALO : HALO + own]
    w1 = first_w[2 : 2 + own]
    r1 = r0 - alpha0 * w1
    sol_ref[...] = alpha0 * r0 + alpha1 * (r1 + beta * r0)
    res_ref[...] = r1 - alpha1 * (w1 - alpha0 * second_w[...] + beta * w1)

    def drain_pair(part, _):
        pair_copy(part).wait_send()
        return 0

    def drain_chip(step, _):
        chip_copy((chip + step) % chips, chip).wait_send()
        return 0

    lax.fori_loop(0, chips, drain_pair, 0)
    lax.fori_loop(1, chips, drain_chip, 0)
    finish_a()
    finish_b()


def body(vols, ctrls, ctrl_coords, vol_coords, sensitivity, vol_lists, ctrl_lists):
    f32 = jnp.float32
    axes = ("vol", "ctrl")
    count = vols * ctrls
    tiles = ctrl_coords.shape[1] // TILE
    own = ctrl_lists.shape[0]
    wide = own + 2 * HALO
    vol_tiles = vol_lists.shape[0]
    first = lax.axis_index(axes) * own

    ids = first + jnp.arange(own, dtype=jnp.int32)
    wanted = ids[:, None] + jnp.arange(-2, 3, dtype=jnp.int32)
    listed = jnp.any(ctrl_lists[:, :, None] == wanted[:, None, :], axis=1) & (wanted >= 0)
    mask = jnp.pad(jnp.where(listed, 0.0, 1e6).astype(f32), ((0, 0), (0, 3)))
    mask = jnp.broadcast_to(mask[:, :, None], (own, 8, TILE))

    doubles = (2.0 * ctrl_coords).reshape(3, tiles, TILE).transpose(1, 0, 2)
    ctrl_pack = jnp.pad(doubles, ((0, 0), (4, 1), (0, 0)))
    points = lax.dynamic_slice_in_dim(jnp.pad(ctrl_pack, ((HALO, HALO), (0, 0), (0, 0))), first, wide, 0)
    vol_pack = jnp.pad((2.0 * vol_coords).reshape(3, vol_tiles, TILE).transpose(1, 0, 2), ((0, 0), (4, 1), (0, 0)))

    shared = lax.axis_size("cases") == 2 and own % 2 == 0 and own // 2 >= HALO
    half = own // 2 if shared else own
    width = half + HALO if shared else wide
    if shared:
        other = lax.ppermute(sensitivity, "cases", [(0, 1), (1, 0)])
        live = (vol_lists >= 0) & (vol_lists // half % 2 == lax.axis_index("cases"))
    else:
        other = jnp.zeros_like(sensitivity)
        live = vol_lists >= 0

    def by_tile(value):
        return jnp.pad(value.reshape(3, vol_tiles, TILE), ((0, 1), (0, 0), (0, 0)))

    grads = jnp.concatenate([by_tile(sensitivity), by_tile(other)], axis=0).transpose(1, 0, 2)
    rank = jnp.cumsum(live.astype(jnp.int32), axis=1) - 1
    slots = jnp.arange(8, dtype=jnp.int32)
    chosen = live[:, :, None] & (rank[:, :, None] == slots)
    lists = jnp.sum(jnp.where(chosen, vol_lists[:, :, None] + 1, 0), axis=1) - 1
    pairs = jnp.sum(live.astype(jnp.int32), axis=1)
    place = jnp.cumsum((pairs > 0).astype(jnp.int32)) - 1
    active = place[-1] + 1
    at = jnp.arange(vol_tiles, dtype=jnp.int32)
    taken = (place[None, :] == at[:, None]) & (pairs > 0)[None, :]
    order = jnp.sum(jnp.where(taken, at[None, :], 0), axis=1)
    sizes = jnp.sum(jnp.where(taken, pairs[None, :], 0), axis=1)
    batches = (jnp.sum(sizes.reshape(-1, GROUP), axis=1) + BATCH - 1) // BATCH
    trips = jnp.where(batches > 0, jnp.maximum(batches, -(-GROUP // AHEAD)), 0)
    trips = jnp.concatenate([trips, active[None]])

    vmem = pl.BlockSpec(memory_space=pltpu.VMEM)
    smem = pl.BlockSpec(memory_space=pltpu.SMEM)
    load_tiles = tiles // own * half + 2 * HALO
    load = pl.pallas_call(
        functools.partial(load_kernel, own, half),
        out_shape=jax.ShapeDtypeStruct((load_tiles, 8, TILE), f32),
        in_specs=[smem, smem, smem, vmem, vmem, vmem],
        out_specs=vmem,
        scratch_shapes=[pltpu.VMEM((GROUP, 3, TILE, TILE), f32)] * 2,
        compiler_params=pltpu.CompilerParams(vmem_limit_bytes=40 * 2**20),
        name="load_terms",
    )(lists.reshape(-1), order, trips, grads, vol_pack, ctrl_pack)

    chips = count // 2
    dma = pltpu.SemaphoreType.DMA
    answer = jax.ShapeDtypeStruct((own, 4, TILE), f32)
    sol, res = pl.pallas_call(
        functools.partial(solve_kernel, vols, ctrls, shared),
        out_shape=(answer, answer),
        in_specs=[vmem, vmem, vmem],
        out_specs=(vmem, vmem),
        scratch_shapes=[
            pltpu.VMEM((chips, width, 8, TILE), f32),
            pltpu.VMEM((chips, width, 8, TILE), f32),
            pltpu.VMEM((chips, width, 8, TILE), f32),
            pltpu.VMEM((width, 8, TILE), f32),
            pltpu.VMEM((width, 4, TILE), f32),
            pltpu.VMEM((2, width, 4, TILE), f32),
            pltpu.VMEM((own + 4, 8, TILE), f32),
            pltpu.VMEM((wide, 3, TILE, TILE), f32),
            pltpu.VMEM((own + 4, KN * 256, TILE), jnp.bfloat16),
            pltpu.VMEM((wide, 16, TILE), jnp.bfloat16),
            pltpu.VMEM((own + 4, 4, TILE), f32),
            pltpu.VMEM((own, 4, TILE), f32),
            pltpu.VMEM((wide, 4, TILE), f32),
            pltpu.VMEM((count, 8, TILE), f32),
            pltpu.VMEM((count, 16, TILE), f32),
            dma((chips,)), dma((chips,)), dma((chips,)), dma((chips,)),
            dma((count,)), dma((count,)), dma((count,)), dma((count,)), dma((1,)), dma((1,)), dma((2,)), dma((2,)),
        ],
        compiler_params=pltpu.CompilerParams(
            collective_id=0, has_side_effects=True, vmem_limit_bytes=40 * 2**20
        ),
        name="scatter_and_solve",
    )(mask, load, points)

    def unpack(value):
        return value.transpose(1, 0, 2)[:3].reshape(3, own * TILE)

    return unpack(sol), unpack(res)


def solution(mesh):
    placed = (
        P(),
        P(None, ("vol", "ctrl")),
        P(None, ("cases", "vol", "ctrl")),
        P(("vol", "ctrl"), None),
        P(("vol", "ctrl"), None),
    )
    return jax.shard_map(
        functools.partial(body, mesh.shape["vol"], mesh.shape["ctrl"]),
        mesh=mesh,
        in_specs=placed,
        out_specs=(P(None, ("cases", "vol", "ctrl")), P(None, ("cases", "vol", "ctrl"))),
        check_vma=False,
    )
```

```python
import functools

import jax
import jax.numpy as jnp
from jax import lax
from jax.experimental import pallas as pl
from jax.experimental.pallas import tpu as pltpu
from jax.sharding import PartitionSpec as P

TILE = 128
KN = 5
BATCH = 16
GROUP = 32
AHEAD = 6
HALO = 4
kernel_weight = 0.03125
MESH = pl.DeviceIdType.MESH


def split_rows(value):
    high = value.astype(jnp.bfloat16).astype(jnp.float32)
    return jnp.concatenate([high, value - high], axis=0)


def phi_tile(columns, rows):
    high, rest = [], []
    for start in range(0, TILE, 32):
        square = None
        for axis in range(3):
            gap = columns(axis, start, 32) - rows[4 + axis : 5 + axis, :]
            square = gap * gap if square is None else square + gap * gap
        ratio = square * lax.rsqrt(jnp.maximum(square, 1e-30))
        margin = jnp.maximum(4.0 - ratio, 0.0)
        twice = margin * margin
        value = twice * twice * (5.0 - margin)
        lead = value.astype(jnp.bfloat16)
        high.append(lead)
        rest.append((value - lead.astype(jnp.float32)).astype(jnp.bfloat16))
    return jnp.concatenate(high + rest, axis=0)


def turn_columns(cols_ref, slot, block):
    for axis in range(3):
        row = block[4 + axis : 5 + axis, :]
        cols_ref[slot, axis] = jnp.broadcast_to(row, (TILE, TILE)).T


def column_reader(cols_ref, slot):
    return lambda axis, start, size: cols_ref[slot, axis, start : start + size, :]


def load_kernel(
    own, half, lists_ref, order_ref, trips_ref, grads_ref, points_ref, ctrl_ref, load_ref, cols_even, cols_odd
):
    load_ref[...] = jnp.zeros_like(load_ref)
    groups = points_ref.shape[0] // GROUP
    active = trips_ref[groups]

    def fill(slot, _):
        turn_columns(cols_even, slot, points_ref[order_ref[slot]])
        return 0

    lax.fori_loop(0, GROUP, fill, 0)

    def visit(group, now, later):
        begin = group * GROUP
        end = jnp.minimum(begin + GROUP, active)
        following = jnp.minimum(group + 1, groups - 1) * GROUP

        def step(index, state):
            tile, entry = state
            for ahead in range(AHEAD):
                slot = jnp.minimum(index * AHEAD + ahead, GROUP - 1)
                turn_columns(later, slot, points_ref[order_ref[following + slot]])
            found = []
            for _ in range(BATCH):
                inside = tile < end
                mine = jnp.maximum(jnp.minimum(tile, end - 1), begin)
                real = order_ref[mine]
                listed = lists_ref[real * 8 + entry]
                more = lists_ref[real * 8 + entry + 1] >= 0
                near = jnp.maximum(listed, 0)
                live = jnp.where(inside & (listed >= 0), 1.0 / 256.0, 0.0).astype(jnp.float32)
                kern = phi_tile(column_reader(now, mine - begin), ctrl_ref[near])
                grads = split_rows(grads_ref[real] * live).astype(jnp.bfloat16)
                both = jnp.concatenate([grads, grads], axis=1)
                place = lax.div(near, own) * half + lax.rem(near, half) + HALO
                found.append((place, jnp.dot(both, kern, preferred_element_type=jnp.float32)))
                tile = jnp.where(inside & jnp.logical_not(more), tile + 1, tile)
                entry = jnp.where(inside & more, entry + 1, 0)
            for place, terms in found:
                load_ref[place] += terms[0:8] + terms[8:16]
            return tile, entry

        lax.fori_loop(0, trips_ref[group], step, (begin, jnp.int32(0)))

    def two(index, _):
        visit(2 * index, cols_even, cols_odd)
        visit(2 * index + 1, cols_odd, cols_even)
        return 0

    lax.fori_loop(0, groups // 2, two, 0)


def solve_kernel(
    vols, ctrls, shared, mask_ref, load_ref, points_ref, sol_ref, res_ref,
    from_pair, to_chip, from_chip, gathered, to_case, parts, away, cols, kern, field, first_w, second_w, start_w, sums_a, sums_b,
    pair_send, pair_recv, chip_send, chip_recv, a_send, a_recv, b_send, b_recv, case_send, case_recv, edge_send, edge_recv,
):
    count = vols * ctrls
    chips = count // 2
    own = sol_ref.shape[0]
    wide = own + 2 * HALO
    vol, ctrl = lax.axis_index("vol"), lax.axis_index("ctrl")
    me = vol * ctrls + ctrl
    chip, core = me // 2, me % 2
    case = lax.axis_index("cases")
    half = own // 2 if shared else own
    width = gathered.shape[0]

    def device(index):
        return {"vol": index // ctrls, "ctrl": index % ctrls}

    barrier = pltpu.get_barrier_semaphore()

    def greet(step, _):
        pl.semaphore_signal(
            barrier, inc=1, device_id=device((me + step) % count), device_id_type=MESH
        )
        return 0

    lax.fori_loop(1, count, greet, 0)
    if shared:
        pl.semaphore_signal(barrier, inc=1, device_id={"cases": 1 - case}, device_id_type=MESH)
    pl.semaphore_wait(barrier, count if shared else count - 1)

    def slab(index):
        return pl.ds(index * half + (HALO - HALO * case if shared else 0), width)

    def pair_copy(part):
        return pltpu.make_async_remote_copy(
            src_ref=load_ref.at[slab(2 * part + 1 - core)],
            dst_ref=from_pair.at[part],
            send_sem=pair_send.at[part],
            recv_sem=pair_recv.at[part],
            device_id=device(2 * chip + 1 - core),
            device_id_type=MESH,
        )

    def chip_copy(part, slot):
        return pltpu.make_async_remote_copy(
            src_ref=to_chip.at[part],
            dst_ref=from_chip.at[slot],
            send_sem=chip_send.at[part],
            recv_sem=chip_recv.at[slot],
            device_id=device(2 * part + core),
            device_id_type=MESH,
        )

    def edge_copy(side):
        return pltpu.make_async_remote_copy(
            src_ref=mask_ref.at[pl.ds((0, own - 2)[side], 2)],
            dst_ref=away.at[pl.ds((own + 2, 0)[side], 2)],
            send_sem=edge_send.at[side],
            recv_sem=edge_recv.at[side],
            device_id=device((me + (count - 1, 1)[side]) % count),
            device_id_type=MESH,
        )

    for side in range(2):
        edge_copy(side).start()
    away[2 : 2 + own] = mask_ref[...]

    def start_pair(step, _):
        pair_copy((chip + step) % chips).start()
        return 0

    lax.fori_loop(1, chips + 1, start_pair, 0)

    def forward(step, _):
        part = (chip + step) % chips
        pair_copy(part).wait_recv()
        to_chip[part] = load_ref[slab(2 * part + core)] + from_pair[part]
        chip_copy(part, chip).start()
        return 0

    lax.fori_loop(1, chips, forward, 0)
    pair_copy(chip).wait_recv()
    gathered[...] = load_ref[slab(me)] + from_pair[chip]

    def turn(row, _):
        turn_columns(cols, row, points_ref[row])
        return 0

    lax.fori_loop(0, KN, turn, 0)

    for side in range(2):
        edge_copy(side).wait()

    def build(row, _):
        for entry in range(KN):
            kern[row, entry * 256 : entry * 256 + 256, :] = phi_tile(
                column_reader(cols, row + entry), points_ref[row + 2] + away[row, entry : entry + 1, :]
            )
        return turn(jnp.minimum(row + KN, wide - 1), 0)

    lax.fori_loop(0, own + HALO, build, 0)

    def gather(step, _):
        part = (chip + step) % chips
        chip_copy(part, part).wait_recv()
        gathered[...] += from_chip[part]
        return 0

    lax.fori_loop(1, chips, gather, 0)

    if shared:
        parts[case] = gathered[:, 0:4]
        to_case[...] = gathered[:, 4:8]
        swap = pltpu.make_async_remote_copy(
            src_ref=to_case,
            dst_ref=parts.at[case],
            send_sem=case_send.at[0],
            recv_sem=case_recv.at[0],
            device_id={"cases": 1 - case},
            device_id_type=MESH,
        )
        swap.start()
        swap.wait()
        start_w[HALO : HALO + half] = parts[0, 0:half]
        start_w[HALO + own : wide] = parts[0, half:width]
        start_w[0:HALO] = parts[1, 0:HALO]
        start_w[HALO + half : HALO + own] = parts[1, HALO:width]
    else:
        start_w[...] = gathered[:, 0:4]

    def spread(source, size):
        value = source[0:size]
        lead = value.astype(jnp.bfloat16).astype(jnp.float32)
        blank = jnp.zeros((size, 8, TILE), jnp.float32)
        field[0:size] = jnp.concatenate([lead, value - lead, blank], axis=1).astype(jnp.bfloat16)

    def apply(source, target, size, shift):
        spread(source, size + 4)
        many = next(k for k in (12, 8, 4) if size % k == 0)

        def body(step, _):
            mixed = []
            for turn in range(many):
                row = step * many + turn
                pieces = []
                for entry in range(KN):
                    pieces += [field[row + entry]] * 2
                mixed.append(
                    jnp.dot(
                        jnp.concatenate(pieces, axis=1),
                        kern[row + shift],
                        preferred_element_type=jnp.float32,
                    )
                )
            for turn in range(many):
                row = step * many + turn
                target[row] = source[row + 2] + kernel_weight / 256.0 * (mixed[turn][0:4] + mixed[turn][4:8])
            return 0

        lax.fori_loop(0, size // many, body, 0)

    def share(sums, send, recv):
        def copy(peer, slot):
            return pltpu.make_async_remote_copy(
                src_ref=sums.at[me],
                dst_ref=sums.at[slot],
                send_sem=send.at[peer],
                recv_sem=recv.at[slot],
                device_id=device(peer),
                device_id_type=MESH,
            )

        def begin(step, _):
            copy((me + step) % count, me).start()
            return 0

        def collect(step, total):
            peer = (me + step) % count
            copy(peer, peer).wait_recv()
            return total + sums[peer]

        def finish(step, _):
            copy((me + step) % count, me).wait_send()
            return 0

        return (
            lambda: lax.fori_loop(1, count, begin, 0),
            lambda: lax.fori_loop(1, count, collect, sums[me]),
            lambda: lax.fori_loop(1, count, finish, 0),
        )

    apply(start_w, first_w, own + 4, 0)
    r0 = start_w[HALO : HALO + own]
    w1 = first_w[2 : 2 + own]
    sums_a[me] = jnp.concatenate([jnp.sum(r0 * r0, axis=0), jnp.sum(r0 * w1, axis=0)], axis=0)
    begin_a, collect_a, finish_a = share(sums_a, a_send, a_recv)
    begin_b, collect_b, finish_b = share(sums_b, b_send, b_recv)
    begin_a()
    apply(first_w, second_w, own, 2)
    total = collect_a()
    rr0, energy0 = jnp.sum(total[0:4]), jnp.sum(total[4:8])
    alpha0 = rr0 / energy0
    r0 = start_w[HALO : HALO + own]
    w1 = first_w[2 : 2 + own]
    r1 = r0 - alpha0 * w1
    image = w1 - alpha0 * second_w[...]
    sums_b[me] = jnp.concatenate(
        [jnp.sum(r1 * r1, axis=0), jnp.sum(r1 * image, axis=0), jnp.sum(r1 * w1, axis=0), jnp.zeros((4, TILE), jnp.float32)],
        axis=0,
    )
    begin_b()
    total = collect_b()
    rr1 = jnp.sum(total[0:4])
    beta = rr1 / rr0
    energy1 = jnp.sum(total[4:8]) + 2.0 * beta * jnp.sum(total[8:12]) + beta * beta * energy0
    alpha1 = rr1 / energy1
    r0 = start_w[HALO : HALO + own]
    w1 = first_w[2 : 2 + own]
    r1 = r0 - alpha0 * w1
    sol_ref[...] = alpha0 * r0 + alpha1 * (r1 + beta * r0)
    res_ref[...] = r1 - alpha1 * (w1 - alpha0 * second_w[...] + beta * w1)

    def drain_pair(part, _):
        pair_copy(part).wait_send()
        return 0

    def drain_chip(step, _):
        chip_copy((chip + step) % chips, chip).wait_send()
        return 0

    lax.fori_loop(0, chips, drain_pair, 0)
    lax.fori_loop(1, chips, drain_chip, 0)
    finish_a()
    finish_b()


def body(vols, ctrls, ctrl_coords, vol_coords, sensitivity, vol_lists, ctrl_lists):
    f32 = jnp.float32
    axes = ("vol", "ctrl")
    count = vols * ctrls
    tiles = ctrl_coords.shape[1] // TILE
    own = ctrl_lists.shape[0]
    wide = own + 2 * HALO
    vol_tiles = vol_lists.shape[0]
    first = lax.axis_index(axes) * own

    ids = first + jnp.arange(own, dtype=jnp.int32)
    wanted = ids[:, None] + jnp.arange(-2, 3, dtype=jnp.int32)
    listed = jnp.any(ctrl_lists[:, :, None] == wanted[:, None, :], axis=1) & (wanted >= 0)
    mask = jnp.pad(jnp.where(listed, 0.0, 1e6).astype(f32), ((0, 0), (0, 3)))
    mask = jnp.broadcast_to(mask[:, :, None], (own, 8, TILE))

    doubles = (2.0 * ctrl_coords).reshape(3, tiles, TILE).transpose(1, 0, 2)
    ctrl_pack = jnp.pad(doubles, ((0, 0), (4, 1), (0, 0)))
    points = lax.dynamic_slice_in_dim(jnp.pad(ctrl_pack, ((HALO, HALO), (0, 0), (0, 0))), first, wide, 0)
    vol_pack = jnp.pad((2.0 * vol_coords).reshape(3, vol_tiles, TILE).transpose(1, 0, 2), ((0, 0), (4, 1), (0, 0)))

    shared = lax.axis_size("cases") == 2 and own % 2 == 0 and own // 2 >= HALO
    half = own // 2 if shared else own
    width = half + HALO if shared else wide
    if shared:
        other = lax.ppermute(sensitivity, "cases", [(0, 1), (1, 0)])
        live = (vol_lists >= 0) & (vol_lists // half % 2 == lax.axis_index("cases"))
    else:
        other = jnp.zeros_like(sensitivity)
        live = vol_lists >= 0

    def by_tile(value):
        return jnp.pad(value.reshape(3, vol_tiles, TILE), ((0, 1), (0, 0), (0, 0)))

    grads = jnp.concatenate([by_tile(sensitivity), by_tile(other)], axis=0).transpose(1, 0, 2)
    rank = jnp.cumsum(live.astype(jnp.int32), axis=1) - 1
    slots = jnp.arange(8, dtype=jnp.int32)
    chosen = live[:, :, None] & (rank[:, :, None] == slots)
    lists = jnp.sum(jnp.where(chosen, vol_lists[:, :, None] + 1, 0), axis=1) - 1
    pairs = jnp.sum(live.astype(jnp.int32), axis=1)
    place = jnp.cumsum((pairs > 0).astype(jnp.int32)) - 1
    active = place[-1] + 1
    at = jnp.arange(vol_tiles, dtype=jnp.int32)
    taken = (place[None, :] == at[:, None]) & (pairs > 0)[None, :]
    order = jnp.sum(jnp.where(taken, at[None, :], 0), axis=1)
    sizes = jnp.sum(jnp.where(taken, pairs[None, :], 0), axis=1)
    batches = (jnp.sum(sizes.reshape(-1, GROUP), axis=1) + BATCH - 1) // BATCH
    trips = jnp.where(batches > 0, jnp.maximum(batches, -(-GROUP // AHEAD)), 0)
    trips = jnp.concatenate([trips, active[None]])

    vmem = pl.BlockSpec(memory_space=pltpu.VMEM)
    smem = pl.BlockSpec(memory_space=pltpu.SMEM)
    load_tiles = tiles // own * half + 2 * HALO
    load = pl.pallas_call(
        functools.partial(load_kernel, own, half),
        out_shape=jax.ShapeDtypeStruct((load_tiles, 8, TILE), f32),
        in_specs=[smem, smem, smem, vmem, vmem, vmem],
        out_specs=vmem,
        scratch_shapes=[pltpu.VMEM((GROUP, 3, TILE, TILE), f32)] * 2,
        compiler_params=pltpu.CompilerParams(vmem_limit_bytes=40 * 2**20),
        name="load_terms",
    )(lists.reshape(-1), order, trips, grads, vol_pack, ctrl_pack)

    chips = count // 2
    dma = pltpu.SemaphoreType.DMA
    answer = jax.ShapeDtypeStruct((own, 4, TILE), f32)
    sol, res = pl.pallas_call(
        functools.partial(solve_kernel, vols, ctrls, shared),
        out_shape=(answer, answer),
        in_specs=[vmem, vmem, vmem],
        out_specs=(vmem, vmem),
        scratch_shapes=[
            pltpu.VMEM((chips, width, 8, TILE), f32),
            pltpu.VMEM((chips, width, 8, TILE), f32),
            pltpu.VMEM((chips, width, 8, TILE), f32),
            pltpu.VMEM((width, 8, TILE), f32),
            pltpu.VMEM((width, 4, TILE), f32),
            pltpu.VMEM((2, width, 4, TILE), f32),
            pltpu.VMEM((own + 4, 8, TILE), f32),
            pltpu.VMEM((wide, 3, TILE, TILE), f32),
            pltpu.VMEM((own + 4, KN * 256, TILE), jnp.bfloat16),
            pltpu.VMEM((wide, 16, TILE), jnp.bfloat16),
            pltpu.VMEM((own + 4, 4, TILE), f32),
            pltpu.VMEM((own, 4, TILE), f32),
            pltpu.VMEM((wide, 4, TILE), f32),
            pltpu.VMEM((count, 8, TILE), f32),
            pltpu.VMEM((count, 16, TILE), f32),
            dma((chips,)), dma((chips,)), dma((chips,)), dma((chips,)),
            dma((count,)), dma((count,)), dma((count,)), dma((count,)), dma((1,)), dma((1,)), dma((2,)), dma((2,)),
        ],
        compiler_params=pltpu.CompilerParams(
            collective_id=0, has_side_effects=True, vmem_limit_bytes=40 * 2**20
        ),
        name="scatter_and_solve",
    )(mask, load, points)

    def unpack(value):
        return value.transpose(1, 0, 2)[:3].reshape(3, own * TILE)

    return unpack(sol), unpack(res)


def solution(mesh):
    placed = (
        P(),
        P(None, ("vol", "ctrl")),
        P(None, ("cases", "vol", "ctrl")),
        P(("vol", "ctrl"), None),
        P(("vol", "ctrl"), None),
    )
    return jax.shard_map(
        functools.partial(body, mesh.shape["vol"], mesh.shape["ctrl"]),
        mesh=mesh,
        in_specs=placed,
        out_specs=(P(None, ("cases", "vol", "ctrl")), P(None, ("cases", "vol", "ctrl"))),
        check_vma=False,
    )
```
